256 devices in a mesh: dp: 8 (over z_hi, core), expert: 32 (over y, x, z_lo).
Axes of the slice: x: 4, y: 4, z: 8 (z_hi: 4, z_lo: 2; z = z_hi * 2 + z_lo), core: 2. Of those that a mesh axis runs over, the one named last changes fastest.
Arguments:
- grad_out: bfloat16 [1024, 3584], P('expert', 'dp'), may hold values from -6 to 6
- routes: int32 [1024, 8], replicated, may hold values from 0 to 31, all different within a row; in each aligned block of 1024 rows (0 to 1023, 1024 to 2047, ...) at most 512 rows name the same one
- gate_probs: float32 [1024, 8], replicated, may hold values from 0.05 to 0.5
- x_rows: bfloat16 [32, 512, 3584], P('expert'), may hold values from -6 to 6
- w_gate: bfloat16 [32, 3584, 2048], P('expert', None, 'dp'), may hold values from -0.09375 to 0.09375
- w_up: bfloat16 [32, 3584, 2048], P('expert', None, 'dp'), may hold values from -0.09375 to 0.09375
- w_down: bfloat16 [32, 2048, 3584], P('expert', 'dp'), may hold values from -0.125 to 0.125
Outputs:
- grad_in: bfloat16 [1024, 3584], P('expert', 'dp')
- grad_gate: bfloat16 [32, 3584, 2048], P('expert', None, 'dp')
- grad_up: bfloat16 [32, 3584, 2048], P('expert', None, 'dp')
- grad_down: bfloat16 [32, 2048, 3584], P('expert', 'dp')
The draws below stay inside these ranges and needn't reach their ends.
Inputs may be any that keep to these rules, and one draw needn't show every extreme that they name: `routes`: each token names 8 different experts; no expert is named by more than 512 tokens, and in every draw some expert is named by exactly 512.
All inputs are finite; a program needn't handle non-finite values.
Results may differ from the reference program's by a relative error of at most 0.0058.
Values may be sent and summed in bfloat16 or wider, within the bound.
No kernel may reach another device: no remote copies, remote signals or barrier semaphores. Data moves between devices by JAX's collectives and lax.ppermute only.
A program may use at most 128 MiB of HBM per device.

```python
import math
import jax
import jax.numpy as jnp
import numpy as np
from jax import lax

D = 3584
FF = 2048
TOP = 8
EXPERTS = 32
TOKENS = 1024
CAP = 512


def block_scale(rng, shape, shards, smallest, largest):
    level = 1.0
    for position, shards_of in shards:
        steps = jax.random.uniform(jax.random.fold_in(jax.random.fold_in(rng, 6), position), (shards_of,), jnp.float32, smallest / len(shards), largest / len(shards))
        level = level * jnp.repeat(jnp.exp(steps), shape[position] // shards_of).reshape((-1,) + (1,) * (len(shape) - 1 - position))
    return level


def assign_block(key, own, number, rows, count, top, most, slope):
    order = jax.random.permutation(key, count)
    packed, ordinary = shares(count, rows * top, most, slope, True), shares(count, rows * top, most, slope, False)
    places = jnp.arange(count)

    def named(tallies, turn):
        used = int((tallies > 0).sum())
        fixed = max(1, used // 4)
        shifted = fixed + (places - fixed + turn * (used - fixed)) % max(1, count - fixed)
        return jnp.zeros((count,), jnp.int32).at[order[jnp.where(places < fixed, places, shifted)]].set(jnp.asarray(tallies, jnp.int32))

    tallies = jnp.where(number % 4 == 0, named(packed, number // 4), named(ordinary, number - number // 4 - 1))
    mixed = jax.random.permutation(jax.random.fold_in(own, 3), count)
    donor, taker = mixed[0:count // 2 * 2:2], mixed[1:count // 2 * 2:2]
    margin = jnp.minimum(tallies[donor] - 1, most - tallies[taker]) // 2
    margin = jnp.where((donor == order[0]) | (taker == order[0]) | (tallies[taker] == 0), 0, jnp.maximum(margin, 0))
    shifted = jax.random.randint(jax.random.fold_in(own, 4), (count // 2,), 0, 1 << 20) % (margin + 1)
    tallies = tallies.at[donor].add(-shifted).at[taker].add(shifted)
    members = jnp.searchsorted(jnp.cumsum(tallies), jnp.arange(rows * top), side="right").astype(jnp.int32)
    table = members.reshape(top, rows).T
    table = table[jax.random.permutation(jax.random.fold_in(own, 1), rows)]
    turn = jax.random.randint(jax.random.fold_in(own, 2), (rows, 1), 0, top)
    return jnp.take_along_axis(table, (jnp.arange(top)[None, :] + turn) % top, axis=1)


def shares(count, total, reach, slope, full):
    portions = [(1 << 20) // math.isqrt(rank ** slope) + 1 for rank in range(1, count + 1)]
    largest = reach if full else min(reach, max(-(-total // count), total * portions[0] // sum(portions)))
    least = 1 if total - largest >= count - 1 else 0
    counts, surplus = [largest] + [least] * (count - 1), total - largest - least * (count - 1)
    while surplus > 0:
        free = [i for i in range(1, count) if counts[i] < largest] or [i for i in range(1, count) if counts[i] < reach]
        pool, left = sum([portions[i] for i in free]), surplus
        for i in free:
            more = min(reach - counts[i], max(1, left * portions[i] // pool), surplus)
            counts[i] = counts[i] + more
            surplus = surplus - more
    return np.array(counts)


def gaussian(stream_key, extent, width, most, cuts=(), kind=jnp.bfloat16):
    result = jax.random.normal(stream_key, extent, jnp.float32) * width
    if len(cuts) > 0:
        result = block_scale(stream_key, extent, cuts, -0.22, 0.18) * result
    return jnp.clip(result, min=-most, max=most).astype(kind)


def setup_inputs(seed: int = 0) -> dict:
    streams_of = jax.random.split(jax.random.key(seed), 8)
    grad_out = gaussian(streams_of[0], (TOKENS, D), 1.0, 6.0, ((0, 32), (1, 8)))
    routes_keys = jax.random.split(jax.random.fold_in(streams_of[1], 1), TOKENS // TOKENS)
    routes_turns = jax.random.permutation(jax.random.fold_in(streams_of[1], 3), TOKENS // TOKENS)
    routes = jax.vmap(lambda own, number: assign_block(jax.random.fold_in(streams_of[1], 2), own, number, TOKENS, EXPERTS, TOP, CAP, 2))(routes_keys, routes_turns).reshape((TOKENS, TOP))
    gate_probs = jnp.clip(jnp.exp(jax.random.uniform(streams_of[2], (TOKENS, TOP), jnp.float32, math.log(0.05), math.log(0.5))), 0.05, 0.5)
    x_rows = gaussian(streams_of[3], (EXPERTS, CAP, D), 1.0, 6.0, ((0, 32),))
    w_gate = gaussian(streams_of[4], (EXPERTS, D, FF), D ** -0.5, 0.09375, ((0, 32), (2, 8)))
    w_up = gaussian(streams_of[5], (EXPERTS, D, FF), D ** -0.5, 0.09375, ((0, 32), (2, 8)))
    w_down = gaussian(streams_of[6], (EXPERTS, FF, D), FF ** -0.5, 0.125, ((0, 32), (1, 8)))
    return {"grad_out": grad_out, "routes": routes, "gate_probs": gate_probs, "x_rows": x_rows, "w_gate": w_gate, "w_up": w_up, "w_down": w_down}


def expert_step(routes, gate_probs, grad_out, carry, inputs):
    expert_id, x_block, gate_mat, up_mat, down_mat = inputs
    chosen = routes == expert_id
    token_hit = jnp.any(chosen, axis=1)
    token_weight = jnp.sum(jnp.where(chosen, gate_probs, jnp.zeros_like(gate_probs)), axis=1)
    rank = jnp.cumsum(token_hit.astype(jnp.int32)) - 1
    slots = jnp.arange(CAP, dtype=jnp.int32)[:, None]
    select = (token_hit[None, :] & (rank[None, :] == slots)).astype(jnp.float32)
    picked = jnp.dot(select, grad_out.astype(jnp.float32), precision=lax.Precision.HIGHEST)
    row_weight = jnp.dot(select, token_weight, precision=lax.Precision.HIGHEST)
    row_grad = (row_weight[:, None] * picked).astype(jnp.bfloat16)
    gate_pre = jnp.dot(x_block, gate_mat, preferred_element_type=jnp.float32)
    up_pre = jnp.dot(x_block, up_mat, preferred_element_type=jnp.float32)
    sigmoid_gate = jax.nn.sigmoid(gate_pre)
    activated = gate_pre * sigmoid_gate
    hidden = (activated * up_pre).astype(jnp.bfloat16)
    hidden_grad = jnp.dot(row_grad, down_mat.T, preferred_element_type=jnp.float32)
    grad_down = jnp.dot(hidden.T, row_grad, preferred_element_type=jnp.float32).astype(jnp.bfloat16)
    gate_grad = (hidden_grad * up_pre * sigmoid_gate * (1.0 + gate_pre * (1.0 - sigmoid_gate))).astype(jnp.bfloat16)
    up_grad = (hidden_grad * activated).astype(jnp.bfloat16)
    grad_gate = jnp.dot(x_block.T, gate_grad, preferred_element_type=jnp.float32).astype(jnp.bfloat16)
    grad_up = jnp.dot(x_block.T, up_grad, preferred_element_type=jnp.float32).astype(jnp.bfloat16)
    input_rows = jnp.dot(gate_grad, gate_mat.T, preferred_element_type=jnp.float32)
    input_rows = input_rows + jnp.dot(up_grad, up_mat.T, preferred_element_type=jnp.float32)
    carry = carry + jnp.dot(select.T, input_rows, precision=lax.Precision.HIGHEST)
    return carry, (grad_gate, grad_up, grad_down)


def reference(grad_out, routes, gate_probs, x_rows, w_gate, w_up, w_down):
    start = jnp.zeros((TOKENS, D), jnp.float32)
    expert_ids = jnp.arange(EXPERTS, dtype=jnp.int32)

    def step(carry, inputs):
        return expert_step(routes, gate_probs, grad_out, carry, inputs)

    total, grads = lax.scan(step, start, (expert_ids, x_rows, w_gate, w_up, w_down))
    return total.astype(jnp.bfloat16), grads[0], grads[1], grads[2]
```

```python
import jax
import jax.numpy as jnp
from jax import lax
from jax.sharding import Mesh, PartitionSpec as P

SHIFTS = (1, 3, 2)
BF = jnp.bfloat16
F32 = jnp.float32


def _line_perm(shift, first):
    pairs = []
    for c in range(2):
        for y in range(4):
            for x in range(4):
                if (c == 0) == first:
                    to = (c * 4 + y) * 4 + (x + shift) % 4
                else:
                    to = (c * 4 + (y + shift) % 4) * 4 + x
                pairs.append(((c * 4 + y) * 4 + x, to))
    return pairs


def _lines(value, shift, first):
    return lax.ppermute(value, ("c", "y", "x"), _line_perm(shift, first))


def _zh(value, shift):
    return lax.ppermute(value, "zh", [(i, (i + shift) % 4) for i in range(4)])


CYCLE = [(0, 1), (1, 3), (3, 2), (2, 0)]
CYCLE_BACK = [(b, a) for a, b in CYCLE]
ACROSS = [(2, 1), (1, 2)]


def _pair(value, pairs):
    return lax.ppermute(value, ("c", "zl"), pairs)


def _core(value):
    return lax.ppermute(value, "c", [(0, 1), (1, 0)])


def _dot(a, b, dims):
    return lax.dot_general(a, b, (dims, ((), ())), preferred_element_type=F32)


def body(grad_out, routes, gate_probs, x_rows, w_gate, w_up, w_down):
    zh, c, y, x, zl = (lax.axis_index(a) for a in ("zh", "c", "y", "x", "zl"))
    home = c == zl
    slots = x_rows.shape[1]

    got = _pair(grad_out, CYCLE)
    far = _pair(grad_out, ACROSS)
    same = jnp.where(home, grad_out, got)
    other = jnp.where(home, got, far)
    pair = jnp.where(
        c == 0, jnp.concatenate([same, other], 1), jnp.concatenate([other, same], 1)
    )
    near = [pair] + [_zh(pair, s) for s in SHIFTS]
    by_shift = {0: near[0], 1: near[1], 3: near[2], 2: near[3]}
    ordered = []
    for k in range(4):
        pick = by_shift[0]
        for s in SHIFTS:
            pick = jnp.where((zh - k) % 4 == s, by_shift[s], pick)
        ordered.append(pick)
    block = jnp.concatenate(ordered, 1)
    line = jnp.concatenate([block] + [_lines(block, s, True) for s in SHIFTS], 0)
    chunks = [line] + [_lines(line, s, False) for s in SHIFTS]

    wd = jnp.concatenate([w_down[0], _core(w_down[0])], 0)
    wg = jnp.concatenate([w_gate[0], _core(w_gate[0])], 1)
    wu = jnp.concatenate([w_up[0], _core(w_up[0])], 1)

    expert_id = (y * 4 + x) * 2 + zl
    chosen = routes == expert_id
    token_hit = jnp.any(chosen, axis=1)
    token_weight = jnp.sum(jnp.where(chosen, gate_probs, jnp.zeros_like(gate_probs)), axis=1)
    rank = jnp.cumsum(token_hit.astype(jnp.int32)) - 1
    rank = jnp.where(token_hit, rank, -1)
    order = jnp.array([0, 3, 1, 2], jnp.int32)

    def arranged(v):
        v = v.reshape(4, 4, 2, 32)
        v = jnp.take(jnp.take(v, (y + order) % 4, axis=0), (x + order) % 4, axis=1)
        zero = v[:, :, 0].reshape(-1)
        one = jnp.swapaxes(v[:, :, 1], 0, 1).reshape(-1)
        return jnp.where(c == 0, zero, one), jnp.where(c == 0, one, zero)

    rank_own, rank_other = arranged(rank)
    weight_own, _ = arranged(token_weight)
    slot = jnp.arange(slots, dtype=jnp.int32)[None, :]
    select_own = (rank_own[:, None] == slot).astype(BF)
    select_other = (rank_other[:, None] == slot).astype(BF)
    xr = x_rows[0]
    x_own = _dot(select_own, xr, ((1,), (0,))).astype(BF)
    x_other = _dot(select_other, xr, ((1,), (0,))).astype(BF)

    gate_pre = _dot(x_own, wg, ((1,), (0,)))
    up_pre = _dot(x_own, wu, ((1,), (0,)))
    sigmoid_gate = jax.nn.sigmoid(gate_pre)
    activated = gate_pre * sigmoid_gate
    hidden = (activated * up_pre).astype(BF)
    slope = up_pre * sigmoid_gate * (1.0 + gate_pre * (1.0 - sigmoid_gate))

    width = 128
    own_sum = None
    back = []
    row_grads, gate_grads, up_grads = [], [], []
    for i, chunk in enumerate(chunks):
        part = slice(i * width, (i + 1) * width)
        row_grad = (weight_own[part, None] * chunk.astype(F32)).astype(BF)
        hidden_grad = _dot(row_grad, wd, ((1,), (1,)))
        gate_grad = (hidden_grad * slope[part]).astype(BF)
        up_grad = (hidden_grad * activated[part]).astype(BF)
        rows = _dot(gate_grad, wg, ((1,), (1,))) + _dot(up_grad, wu, ((1,), (1,)))
        if i == 0:
            own_sum = rows
        else:
            back.append(_lines(rows.astype(BF), -SHIFTS[i - 1], False))
        row_grads.append(row_grad)
        gate_grads.append(gate_grad)
        up_grads.append(up_grad)
    total = own_sum
    for b in back:
        total = total + b.astype(F32)
    result = total[:32]
    sent = total.astype(BF)
    for i, s in enumerate(SHIFTS):
        result = result + _lines(sent[32 * (i + 1) : 32 * (i + 2)], -s, True).astype(F32)
    feats = result.reshape(32, 4, 896)

    def for_zh(k):
        return lax.dynamic_index_in_dim(feats, k % 4, 1, keepdims=False)

    mine = for_zh(zh)
    for s in SHIFTS:
        mine = mine + _zh(for_zh(zh + s).astype(BF), s).astype(F32)
    halves = mine[:, :448], mine[:, 448:]
    same = jnp.where(c == 0, halves[0], halves[1])
    other = jnp.where(c == 0, halves[1], halves[0])
    got = _pair(jnp.where(home, other, same).astype(BF), CYCLE_BACK).astype(F32)
    far = _pair(other.astype(BF), ACROSS).astype(F32)
    grad_in = (jnp.where(home, same, far) + got).astype(BF)

    row_own = jnp.concatenate(row_grads, 0)
    gate_own = jnp.concatenate(gate_grads, 0)
    up_own = jnp.concatenate(up_grads, 0)
    ff = w_gate.shape[2]
    row_all = jnp.concatenate([row_own, _core(row_own)], 0)
    mids = jnp.concatenate([hidden[:, ff:], gate_own[:, ff:], up_own[:, ff:]], 1)
    mids = _core(mids)
    hidden_all = jnp.concatenate([hidden[:, :ff], mids[:, :ff]], 0)
    gate_all = jnp.concatenate([gate_own[:, :ff], mids[:, ff : 2 * ff]], 0)
    up_all = jnp.concatenate([up_own[:, :ff], mids[:, 2 * ff :]], 0)
    x_all = jnp.concatenate([x_own, x_other], 0)
    grad_down = _dot(hidden_all, row_all, ((0,), (0,))).astype(BF)
    grad_gate = _dot(x_all, gate_all, ((0,), (0,))).astype(BF)
    grad_up = _dot(x_all, up_all, ((0,), (0,))).astype(BF)
    return grad_in, grad_gate[None], grad_up[None], grad_down[None]


def solution(mesh):
    fine = Mesh(mesh.devices.reshape(4, 2, 4, 4, 2), ("zh", "c", "y", "x", "zl"))
    expert, dp = ("y", "x", "zl"), ("zh", "c")
    placed = (
        P(expert, dp),
        P(),
        P(),
        P(expert, None, None),
        P(expert, None, dp),
        P(expert, None, dp),
        P(expert, dp, None),
    )
    return jax.shard_map(
        body,
        mesh=fine,
        in_specs=placed,
        out_specs=(
            P(expert, dp),
            P(expert, None, dp),
            P(expert, None, dp),
            P(expert, dp, None),
        ),
        check_vma=False,
    )
```

```python
import functools

import jax
import jax.numpy as jnp
from jax import lax
from jax.experimental import pallas as pl
from jax.experimental.pallas import tpu as pltpu
from jax.sharding import Mesh, PartitionSpec as P

SHIFTS = (1, 3, 2)
BF = jnp.bfloat16
F32 = jnp.float32
SHORT = pl.CostEstimate(flops=0, bytes_accessed=0, transcendentals=0)
LONG = pl.CostEstimate(flops=30_000_000_000, bytes_accessed=0, transcendentals=0)


def _line_perm(shift, first):
    pairs = []
    for c in range(2):
        for y in range(4):
            for x in range(4):
                if (c == 0) == first:
                    to = (c * 4 + y) * 4 + (x + shift) % 4
                else:
                    to = (c * 4 + (y + shift) % 4) * 4 + x
                pairs.append(((c * 4 + y) * 4 + x, to))
    return pairs


def _lines(value, shift, first):
    return lax.ppermute(value, ("c", "y", "x"), _line_perm(shift, first))


def _zh(value, shift):
    return lax.ppermute(value, "zh", [(i, (i + shift) % 4) for i in range(4)])


CYCLE = [(0, 1), (1, 3), (3, 2), (2, 0)]
CYCLE_BACK = [(b, a) for a, b in CYCLE]
ACROSS = [(2, 1), (1, 2)]


def _pair(value, pairs):
    return lax.ppermute(value, ("c", "zl"), pairs)


def _core(value):
    return lax.ppermute(value, "c", [(0, 1), (1, 0)])


def _dot(a, b, dims):
    return lax.dot_general(a, b, (dims, ((), ())), preferred_element_type=F32)


def _route_kernel(place, routes, probs, own, other, weight):
    c, y, x, expert = place[0], place[1], place[2], place[3]
    chosen = routes[...] == expert
    hit = jnp.max(jnp.where(chosen, 1.0, 0.0), axis=0, keepdims=True)
    worth = jnp.sum(jnp.where(chosen, probs[...], 0.0), axis=0, keepdims=True)
    tokens = hit.shape[1]
    natural = lax.broadcasted_iota(jnp.int32, (128, tokens), 1)
    slot = lax.broadcasted_iota(jnp.int32, (128, own.shape[1]), 1)
    row = lax.broadcasted_iota(jnp.int32, (128, 1), 0)
    inner = row // 32
    inner = jnp.where(inner == 1, 3, jnp.where(inner > 1, inner - 1, 0))
    for outer, back in enumerate((0, 2, 3, 1)):
        part = pl.ds(128 * outer, 128)
        for ref, core in ((own, c), (other, 1 - c)):
            ty = (y + jnp.where(core == 0, back, inner)) % 4
            tx = (x + jnp.where(core == 0, inner, back)) % 4
            token = ((ty * 4 + tx) * 2 + core) * 32 + row % 32
            before = jnp.sum(jnp.where(natural < token, hit, 0.0), axis=1, keepdims=True)
            here = natural == token
            named = jnp.sum(jnp.where(here, hit, 0.0), axis=1, keepdims=True)
            rank = jnp.where(named > 0.5, before, -1.0).astype(jnp.int32)
            ref[part, :] = jnp.where(slot == rank, 1.0, 0.0).astype(BF)
            if ref is own:
                weight[part, :] = jnp.sum(jnp.where(here, worth, 0.0), axis=1, keepdims=True)


def _route(place, routes, probs, slots):
    tokens = routes.shape[1]
    half = tokens // 2
    return pl.pallas_call(
        _route_kernel,
        out_shape=(
            jax.ShapeDtypeStruct((half, slots), BF),
            jax.ShapeDtypeStruct((half, slots), BF),
            jax.ShapeDtypeStruct((half, 1), F32),
        ),
        grid=(1,),
        in_specs=[
            pl.BlockSpec(memory_space=pltpu.SMEM),
            pl.BlockSpec(routes.shape, lambda i: (0, 0)),
            pl.BlockSpec(probs.shape, lambda i: (0, 0)),
        ],
        out_specs=[
            pl.BlockSpec((half, slots), lambda i: (0, 0)),
            pl.BlockSpec((half, slots), lambda i: (0, 0)),
            pl.BlockSpec((half, 1), lambda i: (0, 0)),
        ],
        compiler_params=pltpu.CompilerParams(vmem_limit_bytes=16 << 20),
        cost_estimate=SHORT,
    )(place, routes, probs)


def _pair_kernel(tiles, one, two, weight, slope, act, wd0, wd1, wg0, wg1, wu0, wu1, *rest):
    rows1, rows2, row_grad, mid0, mid1, acc = rest[-6:]
    step = pl.program_id(0)
    ff = wd0.shape[0]
    count = one.shape[0]
    flat = ((1,), (1,))

    @pl.when(step == 0)
    def _():
        acc[...] = jnp.zeros_like(acc)

    @pl.when(step < tiles)
    def _():
        both = jnp.concatenate([one[...], two[...]], 0)
        grad = (weight[...] * both.astype(F32)).astype(BF)
        row_grad[...] = grad
        acc[:, :ff] += _dot(grad, wd0[...], flat)
        acc[:, ff:] += _dot(grad, wd1[...], flat)

    @pl.when(step == tiles - 1)
    def _():
        for ref, part in ((mid0, slice(0, ff)), (mid1, slice(ff, 2 * ff))):
            ref[:, :ff] = (acc[:, part] * slope[:, part]).astype(BF)
            ref[:, ff:] = (acc[:, part] * act[:, part]).astype(BF)

    @pl.when(step >= tiles)
    def _():
        total = _dot(mid0[:, :ff], wg0[...], flat) + _dot(mid0[:, ff:], wu0[...], flat)
        total += _dot(mid1[:, :ff], wg1[...], flat) + _dot(mid1[:, ff:], wu1[...], flat)
        rows1[...] = total[:count].astype(rows1.dtype)
        rows2[...] = total[count:].astype(rows2.dtype)


def _pair_step(i, chunks, weight, slope, act, downs, gates, ups, kept):
    count, width = chunks[0].shape
    total, hidden = slope.shape
    ff = hidden // 2
    tile = width // 2
    tiles = width // tile
    down = pl.BlockSpec((ff, tile), lambda s: (0, jnp.minimum(s, tiles - 1)))
    up = pl.BlockSpec((tile, ff), lambda s: (jnp.maximum(s - tiles, 0), 0))
    chunk = pl.BlockSpec((count, tile), lambda s: (0, jnp.minimum(s, tiles - 1)))
    rows = pl.BlockSpec((count, tile), lambda s: (0, jnp.maximum(s - tiles, 0)))
    part = pl.BlockSpec((2 * count, hidden), lambda s: (i, 0))
    any_space = pl.BlockSpec(memory_space=pl.ANY)
    return pl.pallas_call(
        functools.partial(_pair_kernel, tiles),
        grid=(2 * tiles,),
        out_shape=(
            jax.ShapeDtypeStruct((count, width), BF if i else F32),
            jax.ShapeDtypeStruct((count, width), BF),
            jax.ShapeDtypeStruct((total, width), BF),
            jax.ShapeDtypeStruct((total, hidden), BF),
            jax.ShapeDtypeStruct((total, hidden), BF),
        ),
        in_specs=[
            chunk,
            chunk,
            pl.BlockSpec((2 * count, 1), lambda s: (i, 0)),
            part,
            part,
            down,
            down,
            up,
            up,
            up,
            up,
        ]
        + [any_space] * len(kept),
        out_specs=[
            rows,
            rows,
            pl.BlockSpec((2 * count, tile), lambda s: (i, jnp.minimum(s, tiles - 1))),
            part,
            part,
        ],
        scratch_shapes=[pltpu.VMEM((2 * count, hidden), F32)],
        input_output_aliases={11 + k: 2 + k for k in range(len(kept))},
        compiler_params=pltpu.CompilerParams(vmem_limit_bytes=32 << 20),
        cost_estimate=LONG,
    )(*chunks, weight, slope, act, *downs, *gates, *ups, *kept)


def _inputs_kernel(sel_own, sel_other, mid_own, mid_other, x, gate, up, mid):
    @pl.when(pl.program_id(0) == 0)
    def _():
        tokens = ((0,), (0,))
        mid[...] = (
            _dot(sel_own[...], mid_own[...], tokens) + _dot(sel_other[...], mid_other[...], tokens)
        ).astype(BF)

    both = _dot(x[...], mid[...], ((0,), (0,)))
    ff = gate.shape[1]
    gate[...] = both[:, :ff].astype(BF)
    up[...] = both[:, ff:].astype(BF)


def _input_grads(sel_own, sel_other, mid_own, mid_other, xr, ff):
    half, slots = sel_own.shape
    width = xr.shape[1]
    tile = 512
    whole = pl.BlockSpec((half, slots), lambda d: (0, 0))
    mids = pl.BlockSpec((half, 2 * ff), lambda d: (0, 0))
    out = pl.BlockSpec((tile, ff), lambda d: (d, 0))
    return pl.pallas_call(
        _inputs_kernel,
        grid=(width // tile,),
        out_shape=(jax.ShapeDtypeStruct((width, ff), BF),) * 2,
        in_specs=[
            whole,
            whole,
            mids,
            mids,
            pl.BlockSpec((slots, tile), lambda d: (0, d)),
        ],
        out_specs=[out, out],
        scratch_shapes=[pltpu.VMEM((slots, 2 * ff), BF)],
        compiler_params=pltpu.CompilerParams(vmem_limit_bytes=24 << 20),
        cost_estimate=SHORT,
    )(sel_own, sel_other, mid_own, mid_other, xr)


def _down_kernel(hid_own, hid_other, row_own, row_other, out, turned):
    half = hid_own.shape[0]

    @pl.when(pl.program_id(0) == 0)
    def _():
        turned[:, :half] = hid_own[...].T
        turned[:, half:] = hid_other[...].T

    out[...] = (
        _dot(turned[:, :half], row_own[...], ((1,), (0,)))
        + _dot(turned[:, half:], row_other[...], ((1,), (0,)))
    ).astype(BF)


def _down_grad(hidden, mids, row_own, row_other, ff):
    half, width = row_own.shape
    tile = 512
    first = pl.BlockSpec((half, ff), lambda d: (0, 0))
    row = pl.BlockSpec((half, tile), lambda d: (0, d))
    return pl.pallas_call(
        _down_kernel,
        grid=(width // tile,),
        out_shape=jax.ShapeDtypeStruct((ff, width), BF),
        in_specs=[first, first, row, row],
        out_specs=pl.BlockSpec((ff, tile), lambda d: (0, d)),
        scratch_shapes=[pltpu.VMEM((ff, 2 * half), BF)],
        compiler_params=pltpu.CompilerParams(vmem_limit_bytes=16 << 20),
        cost_estimate=SHORT,
    )(hidden, mids, row_own, row_other)


def body(grad_out, routes, gate_probs, x_rows, w_gate, w_up, w_down):
    zh, c, y, x, zl = (lax.axis_index(a) for a in ("zh", "c", "y", "x", "zl"))
    home = c == zl
    slots = x_rows.shape[1]
    ff = w_gate.shape[2]
    barrier = lax.optimization_barrier

    got = _pair(grad_out, CYCLE)
    far = _pair(grad_out, ACROSS)
    same = jnp.where(home, grad_out, got)
    other = jnp.where(home, got, far)
    pair = jnp.where(
        c == 0, jnp.concatenate([same, other], 1), jnp.concatenate([other, same], 1)
    )
    place = jnp.stack([c, y, x, (y * 4 + x) * 2 + zl]).astype(jnp.int32)
    sel_own, sel_other, weight = _route(place, routes.T, gate_probs.T, slots)
    near = [_zh(pair, s) for s in SHIFTS]
    *near, sel_own = barrier((*near, sel_own))
    near = [pair] + near
    by_shift = {0: near[0], 1: near[1], 3: near[2], 2: near[3]}
    ordered = []
    for k in range(4):
        pick = by_shift[0]
        for s in SHIFTS:
            pick = jnp.where((zh - k) % 4 == s, by_shift[s], pick)
        ordered.append(pick)
    block = jnp.concatenate(ordered, 1)
    line = jnp.concatenate([block] + [_lines(block, s, True) for s in SHIFTS], 0)

    gates = w_gate[0], _core(w_gate[0])
    ups = w_up[0], _core(w_up[0])
    downs = w_down[0], _core(w_down[0])
    wg = jnp.concatenate(gates, 1)
    wu = jnp.concatenate(ups, 1)

    xr = x_rows[0]
    x_own = _dot(sel_own, xr, ((1,), (0,))).astype(BF)
    line, x_own = barrier((line, x_own))
    opposite = _lines(line, 2, False)
    gate_pre = _dot(x_own, wg, ((1,), (0,)))
    near_line, gate_pre = barrier((line, gate_pre))
    up_pre = _dot(x_own, wu, ((1,), (0,)))
    sigmoid_gate = jax.nn.sigmoid(gate_pre)
    activated = gate_pre * sigmoid_gate
    hidden = (activated * up_pre).astype(BF)
    slope = up_pre * sigmoid_gate * (1.0 + gate_pre * (1.0 - sigmoid_gate))
    sides = _lines(near_line, 1, False), _lines(near_line, 3, False)

    args = weight, slope, activated, downs, gates, ups
    mine, rows, *kept = _pair_step(0, (line, opposite), *args, ())
    back = [_lines(rows, 2, False)]
    *rows, row_own, mid_own, mid_other = _pair_step(1, sides, *args, kept)
    back += [_lines(rows[0], 3, False), _lines(rows[1], 1, False)]

    row_other = _core(row_own)
    hidden_other = _core(hidden[:, ff:])
    mid_other = _core(mid_other)
    grad_gate, grad_up = _input_grads(sel_own, sel_other, mid_own, mid_other, xr, ff)
    grad_down = _down_grad(hidden, hidden_other, row_own, row_other, ff)

    last, grad_gate, grad_up, grad_down = barrier((back[-1], grad_gate, grad_up, grad_down))
    total = mine
    for b in back[:-1] + [last]:
        total = total + b.astype(F32)
    result = total[:32]
    sent = total.astype(BF)
    for i, s in enumerate(SHIFTS):
        result = result + _lines(sent[32 * (i + 1) : 32 * (i + 2)], -s, True).astype(F32)
    share = result.shape[1] // 4
    quarters = [result[:, k * share : (k + 1) * share] for k in range(4)]

    def for_zh(shift):
        pick = quarters[0]
        for k in range(1, 4):
            pick = jnp.where((zh + shift) % 4 == k, quarters[k], pick)
        return pick

    mine = for_zh(0)
    for s in SHIFTS:
        mine = mine + _zh(for_zh(s).astype(BF), s).astype(F32)
    halves = mine[:, : share // 2], mine[:, share // 2 :]
    same = jnp.where(c == 0, halves[0], halves[1])
    other = jnp.where(c == 0, halves[1], halves[0])
    got = _pair(jnp.where(home, other, same).astype(BF), CYCLE_BACK).astype(F32)
    far = _pair(other.astype(BF), ACROSS).astype(F32)
    grad_in = (jnp.where(home, same, far) + got).astype(BF)
    return grad_in, grad_gate[None], grad_up[None], grad_down[None]


def solution(mesh):
    fine = Mesh(mesh.devices.reshape(4, 2, 4, 4, 2), ("zh", "c", "y", "x", "zl"))
    expert, dp = ("y", "x", "zl"), ("zh", "c")
    placed = (
        P(expert, dp),
        P(),
        P(),
        P(expert, None, None),
        P(expert, None, dp),
        P(expert, None, dp),
        P(expert, dp, None),
    )
    return jax.shard_map(
        body,
        mesh=fine,
        in_specs=placed,
        out_specs=(
            P(expert, dp),
            P(expert, None, dp),
            P(expert, None, dp),
            P(expert, dp, None),
        ),
        check_vma=False,
    )
```

```python
import functools

import jax
import jax.numpy as jnp
from jax import lax
from jax.experimental import pallas as pl
from jax.experimental.pallas import tpu as pltpu
from jax.sharding import Mesh, PartitionSpec as P

SHIFTS = (1, 3, 2)
BF = jnp.bfloat16
F32 = jnp.float32
SHORT = pl.CostEstimate(flops=0, bytes_accessed=0, transcendentals=0)
LONG = pl.CostEstimate(flops=30_000_000_000, bytes_accessed=200_000_000, transcendentals=0)


def _line_perm(shift, first):
    pairs = []
    for c in range(2):
        for y in range(4):
            for x in range(4):
                if (c == 0) == first:
                    to = (c * 4 + y) * 4 + (x + shift) % 4
                else:
                    to = (c * 4 + (y + shift) % 4) * 4 + x
                pairs.append(((c * 4 + y) * 4 + x, to))
    return pairs


def _lines(value, shift, first):
    return lax.ppermute(value, ("c", "y", "x"), _line_perm(shift, first))


def _zh(value, shift):
    return lax.ppermute(value, "zh", [(i, (i + shift) % 4) for i in range(4)])


CYCLE = [(0, 1), (1, 3), (3, 2), (2, 0)]
CYCLE_BACK = [(b, a) for a, b in CYCLE]
ACROSS = [(2, 1), (1, 2)]


def _pair(value, pairs):
    return lax.ppermute(value, ("c", "zl"), pairs)


def _core(value):
    return lax.ppermute(value, "c", [(0, 1), (1, 0)])


def _dot(a, b, dims):
    return lax.dot_general(a, b, (dims, ((), ())), preferred_element_type=F32)


def _route_kernel(place, routes, probs, own, other, weight):
    c, y, x, expert = place[0], place[1], place[2], place[3]
    chosen = routes[...] == expert
    hit = jnp.max(jnp.where(chosen, 1.0, 0.0), axis=0, keepdims=True)
    worth = jnp.sum(jnp.where(chosen, probs[...], 0.0), axis=0, keepdims=True)
    tokens = hit.shape[1]
    natural = lax.broadcasted_iota(jnp.int32, (128, tokens), 1)
    slot = lax.broadcasted_iota(jnp.int32, (128, own.shape[1]), 1)
    row = lax.broadcasted_iota(jnp.int32, (128, 1), 0)
    inner = row // 32
    inner = jnp.where(inner == 1, 3, jnp.where(inner > 1, inner - 1, 0))
    for outer, back in enumerate((0, 2, 3, 1)):
        part = pl.ds(128 * outer, 128)
        for ref, core in ((own, c), (other, 1 - c)):
            ty = (y + jnp.where(core == 0, back, inner)) % 4
            tx = (x + jnp.where(core == 0, inner, back)) % 4
            token = ((ty * 4 + tx) * 2 + core) * 32 + row % 32
            before = jnp.sum(jnp.where(natural < token, hit, 0.0), axis=1, keepdims=True)
            here = natural == token
            named = jnp.sum(jnp.where(here, hit, 0.0), axis=1, keepdims=True)
            rank = jnp.where(named > 0.5, before, -1.0).astype(jnp.int32)
            ref[part, :] = jnp.where(slot == rank, 1.0, 0.0).astype(BF)
            if ref is own:
                weight[part, :] = jnp.sum(jnp.where(here, worth, 0.0), axis=1, keepdims=True)


def _route(place, routes, probs, slots):
    tokens = routes.shape[1]
    half = tokens // 2
    return pl.pallas_call(
        _route_kernel,
        out_shape=(
            jax.ShapeDtypeStruct((half, slots), BF),
            jax.ShapeDtypeStruct((half, slots), BF),
            jax.ShapeDtypeStruct((half, 1), F32),
        ),
        grid=(1,),
        in_specs=[
            pl.BlockSpec(memory_space=pltpu.SMEM),
            pl.BlockSpec(routes.shape, lambda i: (0, 0)),
            pl.BlockSpec(probs.shape, lambda i: (0, 0)),
        ],
        out_specs=[
            pl.BlockSpec((half, slots), lambda i: (0, 0)),
            pl.BlockSpec((half, slots), lambda i: (0, 0)),
            pl.BlockSpec((half, 1), lambda i: (0, 0)),
        ],
        compiler_params=pltpu.CompilerParams(vmem_limit_bytes=16 << 20),
        cost_estimate=SHORT,
    )(place, routes, probs)


def _pair_kernel(tiles, one, two, weight, slope, act, wd0, wd1, wg0, wg1, wu0, wu1, *rest):
    rows1, rows2, row_grad, mid0, mid1, acc = rest[-6:]
    step = pl.program_id(0)
    ff = wd0.shape[0]
    count = one.shape[0]
    flat = ((1,), (1,))

    @pl.when(step == 0)
    def _():
        acc[...] = jnp.zeros_like(acc)

    @pl.when(step < tiles)
    def _():
        both = jnp.concatenate([one[...], two[...]], 0)
        grad = (weight[...] * both.astype(F32)).astype(BF)
        row_grad[...] = grad
        acc[:, :ff] += _dot(grad, wd0[...], flat)
        acc[:, ff:] += _dot(grad, wd1[...], flat)

    @pl.when(step == tiles - 1)
    def _():
        for ref, part in ((mid0, slice(0, ff)), (mid1, slice(ff, 2 * ff))):
            ref[:, :ff] = (acc[:, part] * slope[:, part]).astype(BF)
            ref[:, ff:] = (acc[:, part] * act[:, part]).astype(BF)

    @pl.when(step >= tiles)
    def _():
        total = _dot(mid0[:, :ff], wg0[...], flat) + _dot(mid0[:, ff:], wu0[...], flat)
        total += _dot(mid1[:, :ff], wg1[...], flat) + _dot(mid1[:, ff:], wu1[...], flat)
        rows1[...] = total[:count].astype(rows1.dtype)
        rows2[...] = total[count:].astype(rows2.dtype)


def _pair_step(i, chunks, weight, slope, act, downs, gates, ups, kept):
    count, width = chunks[0].shape
    total, hidden = slope.shape
    ff = hidden // 2
    tile = width // 2
    tiles = width // tile
    down = pl.BlockSpec((ff, tile), lambda s: (0, jnp.minimum(s, tiles - 1)))
    up = pl.BlockSpec((tile, ff), lambda s: (jnp.maximum(s - tiles, 0), 0))
    chunk = pl.BlockSpec((count, tile), lambda s: (0, jnp.minimum(s, tiles - 1)))
    rows = pl.BlockSpec((count, tile), lambda s: (0, jnp.maximum(s - tiles, 0)))
    part = pl.BlockSpec((2 * count, hidden), lambda s: (i, 0))
    any_space = pl.BlockSpec(memory_space=pl.ANY)
    return pl.pallas_call(
        functools.partial(_pair_kernel, tiles),
        grid=(2 * tiles,),
        out_shape=(
            jax.ShapeDtypeStruct((count, width), BF if i else F32),
            jax.ShapeDtypeStruct((count, width), BF),
            jax.ShapeDtypeStruct((total, width), BF),
            jax.ShapeDtypeStruct((total, hidden), BF),
            jax.ShapeDtypeStruct((total, hidden), BF),
        ),
        in_specs=[
            chunk,
            chunk,
            pl.BlockSpec((2 * count, 1), lambda s: (i, 0)),
            part,
            part,
            down,
            down,
            up,
            up,
            up,
            up,
        ]
        + [any_space] * len(kept),
        out_specs=[
            rows,
            rows,
            pl.BlockSpec((2 * count, tile), lambda s: (i, jnp.minimum(s, tiles - 1))),
            part,
            part,
        ],
        scratch_shapes=[pltpu.VMEM((2 * count, hidden), F32)],
        input_output_aliases={11 + k: 2 + k for k in range(len(kept))},
        compiler_params=pltpu.CompilerParams(vmem_limit_bytes=32 << 20),
        cost_estimate=LONG if i else SHORT,
    )(*chunks, weight, slope, act, *downs, *gates, *ups, *kept)


def _inputs_kernel(sel_own, sel_other, mid_own, mid_other, x, gate, up, mid):
    @pl.when(pl.program_id(0) == 0)
    def _():
        tokens = ((0,), (0,))
        mid[...] = (
            _dot(sel_own[...], mid_own[...], tokens) + _dot(sel_other[...], mid_other[...], tokens)
        ).astype(BF)

    both = _dot(x[...], mid[...], ((0,), (0,)))
    ff = gate.shape[1]
    gate[...] = both[:, :ff].astype(BF)
    up[...] = both[:, ff:].astype(BF)


def _input_grads(sel_own, sel_other, mid_own, mid_other, xr, ff):
    half, slots = sel_own.shape
    width = xr.shape[1]
    tile = 512
    whole = pl.BlockSpec((half, slots), lambda d: (0, 0))
    mids = pl.BlockSpec((half, 2 * ff), lambda d: (0, 0))
    out = pl.BlockSpec((tile, ff), lambda d: (d, 0))
    return pl.pallas_call(
        _inputs_kernel,
        grid=(width // tile,),
        out_shape=(jax.ShapeDtypeStruct((width, ff), BF),) * 2,
        in_specs=[
            whole,
            whole,
            mids,
            mids,
            pl.BlockSpec((slots, tile), lambda d: (0, d)),
        ],
        out_specs=[out, out],
        scratch_shapes=[pltpu.VMEM((slots, 2 * ff), BF)],
        compiler_params=pltpu.CompilerParams(vmem_limit_bytes=24 << 20),
        cost_estimate=LONG,
    )(sel_own, sel_other, mid_own, mid_other, xr)


def _down_kernel(hid_own, hid_other, row_own, row_other, out, turned):
    half = hid_own.shape[0]

    @pl.when(pl.program_id(0) == 0)
    def _():
        turned[:, :half] = hid_own[...].T
        turned[:, half:] = hid_other[...].T

    out[...] = (
        _dot(turned[:, :half], row_own[...], ((1,), (0,)))
        + _dot(turned[:, half:], row_other[...], ((1,), (0,)))
    ).astype(BF)


def _down_grad(hidden, mids, row_own, row_other, ff):
    half, width = row_own.shape
    tile = 512
    first = pl.BlockSpec((half, ff), lambda d: (0, 0))
    row = pl.BlockSpec((half, tile), lambda d: (0, d))
    return pl.pallas_call(
        _down_kernel,
        grid=(width // tile,),
        out_shape=jax.ShapeDtypeStruct((ff, width), BF),
        in_specs=[first, first, row, row],
        out_specs=pl.BlockSpec((ff, tile), lambda d: (0, d)),
        scratch_shapes=[pltpu.VMEM((ff, 2 * half), BF)],
        compiler_params=pltpu.CompilerParams(vmem_limit_bytes=16 << 20),
        cost_estimate=LONG,
    )(hidden, mids, row_own, row_other)


def body(grad_out, routes, gate_probs, x_rows, w_gate, w_up, w_down):
    zh, c, y, x, zl = (lax.axis_index(a) for a in ("zh", "c", "y", "x", "zl"))
    home = c == zl
    slots = x_rows.shape[1]
    ff = w_gate.shape[2]
    barrier = lax.optimization_barrier

    got = _pair(grad_out, CYCLE)
    far = _pair(grad_out, ACROSS)
    same = jnp.where(home, grad_out, got)
    other = jnp.where(home, got, far)
    pair = jnp.where(
        c == 0, jnp.concatenate([same, other], 1), jnp.concatenate([other, same], 1)
    )
    gates = w_gate[0], _core(w_gate[0])
    ups = w_up[0], _core(w_up[0])
    downs = w_down[0], _core(w_down[0])

    place = jnp.stack([c, y, x, (y * 4 + x) * 2 + zl]).astype(jnp.int32)
    sel_own, sel_other, weight = _route(place, routes.T, gate_probs.T, slots)
    near = [_zh(pair, s) for s in SHIFTS]
    *near, sel_own = barrier((*near, sel_own))
    near = [pair] + near
    by_shift = {0: near[0], 1: near[1], 3: near[2], 2: near[3]}
    ordered = []
    for k in range(4):
        pick = by_shift[0]
        for s in SHIFTS:
            pick = jnp.where((zh - k) % 4 == s, by_shift[s], pick)
        ordered.append(pick)
    block = jnp.concatenate(ordered, 1)
    line = jnp.concatenate([block] + [_lines(block, s, True) for s in SHIFTS], 0)

    xr = x_rows[0]
    x_own = _dot(sel_own, xr, ((1,), (0,))).astype(BF)
    line, x_own, gates, ups = barrier((line, x_own, gates, ups))
    wg = jnp.concatenate(gates, 1)
    wu = jnp.concatenate(ups, 1)
    opposite = _lines(line, 2, False)
    gate_pre = _dot(x_own, wg, ((1,), (0,)))
    near_line, gate_pre = barrier((line, gate_pre))
    up_pre = _dot(x_own, wu, ((1,), (0,)))
    sigmoid_gate = jax.nn.sigmoid(gate_pre)
    activated = gate_pre * sigmoid_gate
    hidden = (activated * up_pre).astype(BF)
    slope = up_pre * sigmoid_gate * (1.0 + gate_pre * (1.0 - sigmoid_gate))
    sides = _lines(near_line, 1, False), _lines(near_line, 3, False)

    hidden_other = _core(hidden[:, ff:])

    args = weight, slope, activated, downs, gates, ups
    mine, rows, *kept = _pair_step(0, (line, opposite), *args, ())
    rows, hidden_other = barrier((rows, hidden_other))
    back = [_lines(rows, 2, False)]
    *rows, row_own, mid_own, mid_other = _pair_step(1, sides, *args, kept)
    back += [_lines(rows[0], 3, False), _lines(rows[1], 1, False)]

    row_other = _core(row_own)
    mid_other = _core(mid_other)
    total = mine + back[0].astype(F32)
    total, mid_other = barrier((total, mid_other))
    grad_gate, grad_up = _input_grads(sel_own, sel_other, mid_own, mid_other, xr, ff)
    grad_down = _down_grad(hidden, hidden_other, row_own, row_other, ff)

    last, grad_gate, grad_up, grad_down = barrier((back[2], grad_gate, grad_up, grad_down))
    total = total + back[1].astype(F32) + last.astype(F32)
    result = total[:32]
    sent = total.astype(BF)
    for i, s in enumerate(SHIFTS):
        result = result + _lines(sent[32 * (i + 1) : 32 * (i + 2)], -s, True).astype(F32)
    share = result.shape[1] // 4
    quarters = [result[:, k * share : (k + 1) * share] for k in range(4)]

    def for_zh(shift):
        pick = quarters[0]
        for k in range(1, 4):
            pick = jnp.where((zh + shift) % 4 == k, quarters[k], pick)
        return pick

    mine = for_zh(0)
    for s in SHIFTS:
        mine = mine + _zh(for_zh(s).astype(BF), s).astype(F32)
    halves = mine[:, : share // 2], mine[:, share // 2 :]
    same = jnp.where(c == 0, halves[0], halves[1])
    other = jnp.where(c == 0, halves[1], halves[0])
    got = _pair(jnp.where(home, other, same).astype(BF), CYCLE_BACK).astype(F32)
    far = _pair(other.astype(BF), ACROSS).astype(F32)
    grad_in = (jnp.where(home, same, far) + got).astype(BF)
    return grad_in, grad_gate[None], grad_up[None], grad_down[None]


def solution(mesh):
    fine = Mesh(mesh.devices.reshape(4, 2, 4, 4, 2), ("zh", "c", "y", "x", "zl"))
    expert, dp = ("y", "x", "zl"), ("zh", "c")
    placed = (
        P(expert, dp),
        P(),
        P(),
        P(expert, None, None),
        P(expert, None, dp),
        P(expert, None, dp),
        P(expert, dp, None),
    )
    return jax.shard_map(
        body,
        mesh=fine,
        in_specs=placed,
        out_specs=(
            P(expert, dp),
            P(expert, None, dp),
            P(expert, None, dp),
            P(expert, dp, None),
        ),
        check_vma=False,
    )
```

```python
import functools

import jax
import jax.numpy as jnp
from jax import lax
from jax.experimental import pallas as pl
from jax.experimental.pallas import tpu as pltpu
from jax.sharding import Mesh, PartitionSpec as P

SHIFTS = (1, 3, 2)
BF = jnp.bfloat16
F32 = jnp.float32
SHORT = pl.CostEstimate(flops=0, bytes_accessed=0, transcendentals=0)
LONG = pl.CostEstimate(flops=30_000_000_000, bytes_accessed=200_000_000, transcendentals=0)


def _line_perm(shift, first):
    pairs = []
    for c in range(2):
        for y in range(4):
            for x in range(4):
                if (c == 0) == first:
                    to = (c * 4 + y) * 4 + (x + shift) % 4
                else:
                    to = (c * 4 + (y + shift) % 4) * 4 + x
                pairs.append(((c * 4 + y) * 4 + x, to))
    return pairs


def _lines(value, shift, first):
    return lax.ppermute(value, ("c", "y", "x"), _line_perm(shift, first))


def _zh(value, shift):
    return lax.ppermute(value, "zh", [(i, (i + shift) % 4) for i in range(4)])


CYCLE = [(0, 1), (1, 3), (3, 2), (2, 0)]
CYCLE_BACK = [(b, a) for a, b in CYCLE]
ACROSS = [(2, 1), (1, 2)]


def _pair(value, pairs):
    return lax.ppermute(value, ("c", "zl"), pairs)


def _core(value):
    return lax.ppermute(value, "c", [(0, 1), (1, 0)])


def _dot(a, b, dims):
    return lax.dot_general(a, b, (dims, ((), ())), preferred_element_type=F32)


def _route_kernel(place, routes, probs, own, other, weight):
    c, y, x, expert = place[0], place[1], place[2], place[3]
    chosen = routes[...] == expert
    hit = jnp.max(jnp.where(chosen, 1.0, 0.0), axis=0, keepdims=True)
    worth = jnp.sum(jnp.where(chosen, probs[...], 0.0), axis=0, keepdims=True)
    tokens = hit.shape[1]
    natural = lax.broadcasted_iota(jnp.int32, (128, tokens), 1)
    slot = lax.broadcasted_iota(jnp.int32, (128, own.shape[1]), 1)
    row = lax.broadcasted_iota(jnp.int32, (128, 1), 0)
    inner = row // 32
    inner = jnp.where(inner == 1, 3, jnp.where(inner > 1, inner - 1, 0))
    for outer, back in enumerate((0, 2, 3, 1)):
        part = pl.ds(128 * outer, 128)
        for ref, core in ((own, c), (other, 1 - c)):
            ty = (y + jnp.where(core == 0, back, inner)) % 4
            tx = (x + jnp.where(core == 0, inner, back)) % 4
            token = ((ty * 4 + tx) * 2 + core) * 32 + row % 32
            before = jnp.sum(jnp.where(natural < token, hit, 0.0), axis=1, keepdims=True)
            here = natural == token
            named = jnp.sum(jnp.where(here, hit, 0.0), axis=1, keepdims=True)
            rank = jnp.where(named > 0.5, before, -1.0).astype(jnp.int32)
            ref[part, :] = jnp.where(slot == rank, 1.0, 0.0).astype(BF)
            if ref is own:
                weight[part, :] = jnp.sum(jnp.where(here, worth, 0.0), axis=1, keepdims=True)


def _route(place, routes, probs, slots):
    tokens = routes.shape[1]
    half = tokens // 2
    return pl.pallas_call(
        _route_kernel,
        out_shape=(
            jax.ShapeDtypeStruct((half, slots), BF),
            jax.ShapeDtypeStruct((half, slots), BF),
            jax.ShapeDtypeStruct((half, 1), F32),
        ),
        grid=(1,),
        in_specs=[
            pl.BlockSpec(memory_space=pltpu.SMEM),
            pl.BlockSpec(routes.shape, lambda i: (0, 0)),
            pl.BlockSpec(probs.shape, lambda i: (0, 0)),
        ],
        out_specs=[
            pl.BlockSpec((half, slots), lambda i: (0, 0)),
            pl.BlockSpec((half, slots), lambda i: (0, 0)),
            pl.BlockSpec((half, 1), lambda i: (0, 0)),
        ],
        compiler_params=pltpu.CompilerParams(vmem_limit_bytes=16 << 20),
        cost_estimate=SHORT,
    )(place, routes, probs)


def _pair_kernel(tiles, one, two, weight, slope, act, wd0, wd1, wg0, wg1, wu0, wu1, *rest):
    rows1, rows2, row_grad, mid0, mid1, acc = rest[-6:]
    step = pl.program_id(0)
    ff = wd0.shape[0]
    count = one.shape[0]
    flat = ((1,), (1,))

    @pl.when(step == 0)
    def _():
        acc[...] = jnp.zeros_like(acc)

    @pl.when(step < tiles)
    def _():
        both = jnp.concatenate([one[...], two[...]], 0)
        grad = (weight[...] * both.astype(F32)).astype(BF)
        row_grad[...] = grad
        acc[:, :ff] += _dot(grad, wd0[...], flat)
        acc[:, ff:] += _dot(grad, wd1[...], flat)

    @pl.when(step == tiles - 1)
    def _():
        for ref, part in ((mid0, slice(0, ff)), (mid1, slice(ff, 2 * ff))):
            ref[:, :ff] = (acc[:, part] * slope[:, part]).astype(BF)
            ref[:, ff:] = (acc[:, part] * act[:, part]).astype(BF)

    @pl.when(step >= tiles)
    def _():
        total = _dot(mid0[:, :ff], wg0[...], flat) + _dot(mid0[:, ff:], wu0[...], flat)
        total += _dot(mid1[:, :ff], wg1[...], flat) + _dot(mid1[:, ff:], wu1[...], flat)
        rows1[...] = total[:count].astype(rows1.dtype)
        rows2[...] = total[count:].astype(rows2.dtype)


def _pair_step(i, chunks, weight, slope, act, downs, gates, ups, kept):
    count, width = chunks[0].shape
    total, hidden = slope.shape
    ff = hidden // 2
    tile = width // 2
    tiles = width // tile
    down = pl.BlockSpec((ff, tile), lambda s: (0, jnp.minimum(s, tiles - 1)))
    up = pl.BlockSpec((tile, ff), lambda s: (jnp.maximum(s - tiles, 0), 0))
    chunk = pl.BlockSpec((count, tile), lambda s: (0, jnp.minimum(s, tiles - 1)))
    rows = pl.BlockSpec((count, tile), lambda s: (0, jnp.maximum(s - tiles, 0)))
    part = pl.BlockSpec((2 * count, hidden), lambda s: (i, 0))
    any_space = pl.BlockSpec(memory_space=pl.ANY)
    return pl.pallas_call(
        functools.partial(_pair_kernel, tiles),
        grid=(2 * tiles,),
        out_shape=(
            jax.ShapeDtypeStruct((count, width), BF if i else F32),
            jax.ShapeDtypeStruct((count, width), BF),
            jax.ShapeDtypeStruct((total, width), BF),
            jax.ShapeDtypeStruct((total, hidden), BF),
            jax.ShapeDtypeStruct((total, hidden), BF),
        ),
        in_specs=[
            chunk,
            chunk,
            pl.BlockSpec((2 * count, 1), lambda s: (i, 0)),
            part,
            part,
            down,
            down,
            up,
            up,
            up,
            up,
        ]
        + [any_space] * len(kept),
        out_specs=[
            rows,
            rows,
            pl.BlockSpec((2 * count, tile), lambda s: (i, jnp.minimum(s, tiles - 1))),
            part,
            part,
        ],
        scratch_shapes=[pltpu.VMEM((2 * count, hidden), F32)],
        input_output_aliases={11 + k: 2 + k for k in range(len(kept))},
        compiler_params=pltpu.CompilerParams(vmem_limit_bytes=32 << 20),
        cost_estimate=LONG if i else SHORT,
    )(*chunks, weight, slope, act, *downs, *gates, *ups, *kept)


def _inputs_kernel(sel_own, sel_other, mid_own, mid_other, x, gate, up, mid):
    @pl.when(pl.program_id(0) == 0)
    def _():
        tokens = ((0,), (0,))
        mid[...] = (
            _dot(sel_own[...], mid_own[...], tokens) + _dot(sel_other[...], mid_other[...], tokens)
        ).astype(BF)

    both = _dot(x[...], mid[...], ((0,), (0,)))
    ff = gate.shape[1]
    gate[...] = both[:, :ff].astype(BF)
    up[...] = both[:, ff:].astype(BF)


def _input_grads(sel_own, sel_other, mid_own, mid_other, xr, ff):
    half, slots = sel_own.shape
    width = xr.shape[1]
    tile = 896
    whole = pl.BlockSpec((half, slots), lambda d: (0, 0))
    mids = pl.BlockSpec((half, 2 * ff), lambda d: (0, 0))
    out = pl.BlockSpec((tile, ff), lambda d: (d, 0))
    return pl.pallas_call(
        _inputs_kernel,
        grid=(width // tile,),
        out_shape=(jax.ShapeDtypeStruct((width, ff), BF),) * 2,
        in_specs=[
            whole,
            whole,
            mids,
            mids,
            pl.BlockSpec((slots, tile), lambda d: (0, d)),
        ],
        out_specs=[out, out],
        scratch_shapes=[pltpu.VMEM((slots, 2 * ff), BF)],
        compiler_params=pltpu.CompilerParams(vmem_limit_bytes=24 << 20),
        cost_estimate=LONG,
    )(sel_own, sel_other, mid_own, mid_other, xr)


def _down_kernel(hid_own, hid_other, row_own, row_other, out, turned):
    half = hid_own.shape[0]

    @pl.when(pl.program_id(0) == 0)
    def _():
        turned[:, :half] = hid_own[...].T
        turned[:, half:] = hid_other[...].T

    out[...] = (
        _dot(turned[:, :half], row_own[...], ((1,), (0,)))
        + _dot(turned[:, half:], row_other[...], ((1,), (0,)))
    ).astype(BF)


def _down_grad(hidden, mids, row_own, row_other, ff):
    half, width = row_own.shape
    tile = 896
    first = pl.BlockSpec((half, ff), lambda d: (0, 0))
    row = pl.BlockSpec((half, tile), lambda d: (0, d))
    return pl.pallas_call(
        _down_kernel,
        grid=(width // tile,),
        out_shape=jax.ShapeDtypeStruct((ff, width), BF),
        in_specs=[first, first, row, row],
        out_specs=pl.BlockSpec((ff, tile), lambda d: (0, d)),
        scratch_shapes=[pltpu.VMEM((ff, 2 * half), BF)],
        compiler_params=pltpu.CompilerParams(vmem_limit_bytes=16 << 20),
        cost_estimate=LONG,
    )(hidden, mids, row_own, row_other)


def body(grad_out, routes, gate_probs, x_rows, w_gate, w_up, w_down):
    zh, c, y, x, zl = (lax.axis_index(a) for a in ("zh", "c", "y", "x", "zl"))
    home = c == zl
    slots = x_rows.shape[1]
    ff = w_gate.shape[2]
    barrier = lax.optimization_barrier

    got = _pair(grad_out, CYCLE)
    far = _pair(grad_out, ACROSS)
    same = jnp.where(home, grad_out, got)
    other = jnp.where(home, got, far)
    pair = jnp.where(
        c == 0, jnp.concatenate([same, other], 1), jnp.concatenate([other, same], 1)
    )
    gates = w_gate[0], _core(w_gate[0])
    ups = w_up[0], _core(w_up[0])
    downs = w_down[0], _core(w_down[0])

    place = jnp.stack([c, y, x, (y * 4 + x) * 2 + zl]).astype(jnp.int32)
    sel_own, sel_other, weight = _route(place, routes.T, gate_probs.T, slots)
    near = [_zh(pair, s) for s in SHIFTS]
    *near, sel_own = barrier((*near, sel_own))
    near = [pair] + near
    by_shift = {0: near[0], 1: near[1], 3: near[2], 2: near[3]}
    ordered = []
    for k in range(4):
        pick = by_shift[0]
        for s in SHIFTS:
            pick = jnp.where((zh - k) % 4 == s, by_shift[s], pick)
        ordered.append(pick)
    block = jnp.concatenate(ordered, 1)
    line = jnp.concatenate([block] + [_lines(block, s, True) for s in SHIFTS], 0)

    xr = x_rows[0]
    x_own = _dot(sel_own, xr, ((1,), (0,))).astype(BF)
    line, x_own, gates, ups = barrier((line, x_own, gates, ups))
    wg = jnp.concatenate(gates, 1)
    wu = jnp.concatenate(ups, 1)
    opposite = _lines(line, 2, False)
    gate_pre = _dot(x_own, wg, ((1,), (0,)))
    near_line, gate_pre = barrier((line, gate_pre))
    up_pre = _dot(x_own, wu, ((1,), (0,)))
    sigmoid_gate = jax.nn.sigmoid(gate_pre)
    activated = gate_pre * sigmoid_gate
    hidden = (activated * up_pre).astype(BF)
    slope = up_pre * sigmoid_gate * (1.0 + gate_pre * (1.0 - sigmoid_gate))
    sides = _lines(near_line, 1, False), _lines(near_line, 3, False)

    hidden_other = _core(hidden[:, ff:])

    args = weight, slope, activated, downs, gates, ups
    mine, rows, *kept = _pair_step(0, (line, opposite), *args, ())
    rows, hidden_other = barrier((rows, hidden_other))
    back = [_lines(rows, 2, False)]
    *rows, row_own, mid_own, mid_other = _pair_step(1, sides, *args, kept)
    back += [_lines(rows[0], 3, False), _lines(rows[1], 1, False)]

    row_other = _core(row_own)
    mid_other = _core(mid_other)
    total = mine + back[0].astype(F32)
    total, mid_other = barrier((total, mid_other))
    grad_gate, grad_up = _input_grads(sel_own, sel_other, mid_own, mid_other, xr, ff)
    grad_down = _down_grad(hidden, hidden_other, row_own, row_other, ff)

    last, grad_gate, grad_up, grad_down = barrier((back[2], grad_gate, grad_up, grad_down))

    def added(part):
        return total[part] + back[1][part].astype(F32) + last[part].astype(F32)

    result = added(slice(0, 32))
    sent = added(slice(32, None)).astype(BF)
    for i, s in enumerate(SHIFTS):
        result = result + _lines(sent[32 * i : 32 * (i + 1)], -s, True).astype(F32)
    share = result.shape[1] // 4
    quarters = [result[:, k * share : (k + 1) * share] for k in range(4)]

    def for_zh(shift):
        pick = quarters[0]
        for k in range(1, 4):
            pick = jnp.where((zh + shift) % 4 == k, quarters[k], pick)
        return pick

    mine = for_zh(0)
    for s in SHIFTS:
        mine = mine + _zh(for_zh(s).astype(BF), s).astype(F32)
    halves = mine[:, : share // 2], mine[:, share // 2 :]
    same = jnp.where(c == 0, halves[0], halves[1])
    other = jnp.where(c == 0, halves[1], halves[0])
    got = _pair(jnp.where(home, other, same).astype(BF), CYCLE_BACK).astype(F32)
    far = _pair(other.astype(BF), ACROSS).astype(F32)
    grad_in = (jnp.where(home, same, far) + got).astype(BF)
    return grad_in, grad_gate[None], grad_up[None], grad_down[None]


def solution(mesh):
    fine = Mesh(mesh.devices.reshape(4, 2, 4, 4, 2), ("zh", "c", "y", "x", "zl"))
    expert, dp = ("y", "x", "zl"), ("zh", "c")
    placed = (
        P(expert, dp),
        P(),
        P(),
        P(expert, None, None),
        P(expert, None, dp),
        P(expert, None, dp),
        P(expert, dp, None),
    )
    return jax.shard_map(
        body,
        mesh=fine,
        in_specs=placed,
        out_specs=(
            P(expert, dp),
            P(expert, None, dp),
            P(expert, None, dp),
            P(expert, dp, None),
        ),
        check_vma=False,
    )
```

```python
import functools

import jax
import jax.numpy as jnp
from jax import lax
from jax.experimental import pallas as pl
from jax.experimental.pallas import tpu as pltpu
from jax.sharding import Mesh, PartitionSpec as P

SHIFTS = (1, 3, 2)
BF = jnp.bfloat16
F32 = jnp.float32
SHORT = pl.CostEstimate(flops=0, bytes_accessed=0, transcendentals=0)
LONG = pl.CostEstimate(flops=30_000_000_000, bytes_accessed=200_000_000, transcendentals=0)


def _line_perm(shift, first):
    pairs = []
    for c in range(2):
        for y in range(4):
            for x in range(4):
                if (c == 0) == first:
                    to = (c * 4 + y) * 4 + (x + shift) % 4
                else:
                    to = (c * 4 + (y + shift) % 4) * 4 + x
                pairs.append(((c * 4 + y) * 4 + x, to))
    return pairs


def _lines(value, shift, first):
    return lax.ppermute(value, ("c", "y", "x"), _line_perm(shift, first))


def _zh(value, shift):
    return lax.ppermute(value, "zh", [(i, (i + shift) % 4) for i in range(4)])


CYCLE = [(0, 1), (1, 3), (3, 2), (2, 0)]
CYCLE_BACK = [(b, a) for a, b in CYCLE]
ACROSS = [(2, 1), (1, 2)]


def _pair(value, pairs):
    return lax.ppermute(value, ("c", "zl"), pairs)


def _core(value):
    return lax.ppermute(value, "c", [(0, 1), (1, 0)])


def _dot(a, b, dims):
    return lax.dot_general(a, b, (dims, ((), ())), preferred_element_type=F32)


def _route_kernel(place, routes, probs, own, other, weight):
    c, y, x, expert = place[0], place[1], place[2], place[3]
    chosen = routes[...] == expert
    hit = jnp.max(jnp.where(chosen, 1.0, 0.0), axis=0, keepdims=True)
    worth = jnp.sum(jnp.where(chosen, probs[...], 0.0), axis=0, keepdims=True)
    tokens = hit.shape[1]
    natural = lax.broadcasted_iota(jnp.int32, (128, tokens), 1)
    slot = lax.broadcasted_iota(jnp.int32, (128, own.shape[1]), 1)
    row = lax.broadcasted_iota(jnp.int32, (128, 1), 0)
    inner = row // 32
    inner = jnp.where(inner == 1, 3, jnp.where(inner > 1, inner - 1, 0))
    for outer, back in enumerate((0, 2, 3, 1)):
        part = pl.ds(128 * outer, 128)
        for ref, core in ((own, c), (other, 1 - c)):
            ty = (y + jnp.where(core == 0, back, inner)) % 4
            tx = (x + jnp.where(core == 0, inner, back)) % 4
            token = ((ty * 4 + tx) * 2 + core) * 32 + row % 32
            before = jnp.sum(jnp.where(natural < token, hit, 0.0), axis=1, keepdims=True)
            here = natural == token
            named = jnp.sum(jnp.where(here, hit, 0.0), axis=1, keepdims=True)
            rank = jnp.where(named > 0.5, before, -1.0).astype(jnp.int32)
            ref[part, :] = jnp.where(slot == rank, 1.0, 0.0).astype(BF)
            if ref is own:
                weight[part, :] = jnp.sum(jnp.where(here, worth, 0.0), axis=1, keepdims=True)


def _route(place, routes, probs, slots):
    tokens = routes.shape[1]
    half = tokens // 2
    return pl.pallas_call(
        _route_kernel,
        out_shape=(
            jax.ShapeDtypeStruct((half, slots), BF),
            jax.ShapeDtypeStruct((half, slots), BF),
            jax.ShapeDtypeStruct((half, 1), F32),
        ),
        grid=(1,),
        in_specs=[
            pl.BlockSpec(memory_space=pltpu.SMEM),
            pl.BlockSpec(routes.shape, lambda i: (0, 0)),
            pl.BlockSpec(probs.shape, lambda i: (0, 0)),
        ],
        out_specs=[
            pl.BlockSpec((half, slots), lambda i: (0, 0)),
            pl.BlockSpec((half, slots), lambda i: (0, 0)),
            pl.BlockSpec((half, 1), lambda i: (0, 0)),
        ],
        compiler_params=pltpu.CompilerParams(vmem_limit_bytes=16 << 20),
        cost_estimate=SHORT,
    )(place, routes, probs)


def _pair_kernel(tiles, one, two, weight, slope, act, wd0, wd1, wg0, wg1, wu0, wu1, *rest):
    rows1, rows2, row_grad, mid0, mid1, acc = rest[-6:]
    step = pl.program_id(0)
    ff = wd0.shape[0]
    count = one.shape[0]
    flat = ((1,), (1,))

    @pl.when(step == 0)
    def _():
        acc[...] = jnp.zeros_like(acc)

    @pl.when(step < tiles)
    def _():
        both = jnp.concatenate([one[...], two[...]], 0)
        grad = (weight[...] * both.astype(F32)).astype(BF)
        row_grad[...] = grad
        acc[:, :ff] += _dot(grad, wd0[...], flat)
        acc[:, ff:] += _dot(grad, wd1[...], flat)

    @pl.when(step == tiles - 1)
    def _():
        for ref, part in ((mid0, slice(0, ff)), (mid1, slice(ff, 2 * ff))):
            ref[:, :ff] = (acc[:, part] * slope[:, part]).astype(BF)
            ref[:, ff:] = (acc[:, part] * act[:, part]).astype(BF)

    @pl.when(step >= tiles)
    def _():
        total = _dot(mid0[:, :ff], wg0[...], flat) + _dot(mid0[:, ff:], wu0[...], flat)
        total += _dot(mid1[:, :ff], wg1[...], flat) + _dot(mid1[:, ff:], wu1[...], flat)
        rows1[...] = total[:count].astype(rows1.dtype)
        rows2[...] = total[count:].astype(rows2.dtype)


def _pair_step(i, chunks, weight, slope, act, downs, gates, ups, kept):
    count, width = chunks[0].shape
    total, hidden = slope.shape
    ff = hidden // 2
    tile = width // 2
    tiles = width // tile
    down = pl.BlockSpec((ff, tile), lambda s: (0, jnp.minimum(s, tiles - 1)))
    up = pl.BlockSpec((tile, ff), lambda s: (jnp.maximum(s - tiles, 0), 0))
    chunk = pl.BlockSpec((count, tile), lambda s: (0, jnp.minimum(s, tiles - 1)))
    rows = pl.BlockSpec((count, tile), lambda s: (0, jnp.maximum(s - tiles, 0)))
    part = pl.BlockSpec((2 * count, hidden), lambda s: (i, 0))
    any_space = pl.BlockSpec(memory_space=pl.ANY)
    return pl.pallas_call(
        functools.partial(_pair_kernel, tiles),
        grid=(2 * tiles,),
        out_shape=(
            jax.ShapeDtypeStruct((count, width), BF if i else F32),
            jax.ShapeDtypeStruct((count, width), BF),
            jax.ShapeDtypeStruct((total, width), BF),
            jax.ShapeDtypeStruct((total, hidden), BF),
            jax.ShapeDtypeStruct((total, hidden), BF),
        ),
        in_specs=[
            chunk,
            chunk,
            pl.BlockSpec((2 * count, 1), lambda s: (i, 0)),
            part,
            part,
            down,
            down,
            up,
            up,
            up,
            up,
        ]
        + [any_space] * len(kept),
        out_specs=[
            rows,
            rows,
            pl.BlockSpec((2 * count, tile), lambda s: (i, jnp.minimum(s, tiles - 1))),
            part,
            part,
        ],
        scratch_shapes=[pltpu.VMEM((2 * count, hidden), F32)],
        input_output_aliases={11 + k: 2 + k for k in range(len(kept))},
        compiler_params=pltpu.CompilerParams(vmem_limit_bytes=32 << 20),
        cost_estimate=LONG if i else SHORT,
    )(*chunks, weight, slope, act, *downs, *gates, *ups, *kept)


def _inputs_kernel(sel_own, sel_other, mid_own, mid_other, x, gate, up, mid):
    @pl.when(pl.program_id(0) == 0)
    def _():
        tokens = ((0,), (0,))
        mid[...] = (
            _dot(sel_own[...], mid_own[...], tokens) + _dot(sel_other[...], mid_other[...], tokens)
        ).astype(BF)

    both = _dot(x[...], mid[...], ((0,), (0,)))
    ff = gate.shape[1]
    gate[...] = both[:, :ff].astype(BF)
    up[...] = both[:, ff:].astype(BF)


def _input_grads(sel_own, sel_other, mid_own, mid_other, xr, ff):
    half, slots = sel_own.shape
    width = xr.shape[1]
    tile = 896
    whole = pl.BlockSpec((half, slots), lambda d: (0, 0))
    mids = pl.BlockSpec((half, 2 * ff), lambda d: (0, 0))
    out = pl.BlockSpec((tile, ff), lambda d: (d, 0))
    return pl.pallas_call(
        _inputs_kernel,
        grid=(width // tile,),
        out_shape=(jax.ShapeDtypeStruct((width, ff), BF),) * 2,
        in_specs=[
            whole,
            whole,
            mids,
            mids,
            pl.BlockSpec((slots, tile), lambda d: (0, d)),
        ],
        out_specs=[out, out],
        scratch_shapes=[pltpu.VMEM((slots, 2 * ff), BF)],
        compiler_params=pltpu.CompilerParams(vmem_limit_bytes=24 << 20),
        cost_estimate=LONG,
    )(sel_own, sel_other, mid_own, mid_other, xr)


def _down_kernel(hid_own, hid_other, row_own, row_other, out, turned):
    half = hid_own.shape[0]

    @pl.when(pl.program_id(0) == 0)
    def _():
        turned[:, :half] = hid_own[...].T
        turned[:, half:] = hid_other[...].T

    out[...] = (
        _dot(turned[:, :half], row_own[...], ((1,), (0,)))
        + _dot(turned[:, half:], row_other[...], ((1,), (0,)))
    ).astype(BF)


def _down_grad(hidden, mids, row_own, row_other, ff):
    half, width = row_own.shape
    tile = 896
    first = pl.BlockSpec((half, ff), lambda d: (0, 0))
    row = pl.BlockSpec((half, tile), lambda d: (0, d))
    return pl.pallas_call(
        _down_kernel,
        grid=(width // tile,),
        out_shape=jax.ShapeDtypeStruct((ff, width), BF),
        in_specs=[first, first, row, row],
        out_specs=pl.BlockSpec((ff, tile), lambda d: (0, d)),
        scratch_shapes=[pltpu.VMEM((ff, 2 * half), BF)],
        compiler_params=pltpu.CompilerParams(vmem_limit_bytes=16 << 20),
        cost_estimate=LONG,
    )(hidden, mids, row_own, row_other)


def body(grad_out, routes, gate_probs, x_rows, w_gate, w_up, w_down):
    zh, c, y, x, zl = (lax.axis_index(a) for a in ("zh", "c", "y", "x", "zl"))
    home = c == zl
    slots = x_rows.shape[1]
    ff = w_gate.shape[2]
    barrier = lax.optimization_barrier

    got = _pair(grad_out, CYCLE)
    far = _pair(grad_out, ACROSS)
    same = jnp.where(home, grad_out, got)
    other = jnp.where(home, got, far)
    pair = jnp.where(
        c == 0, jnp.concatenate([same, other], 1), jnp.concatenate([other, same], 1)
    )
    gates = w_gate[0], _core(w_gate[0])
    ups = w_up[0], _core(w_up[0])
    downs = w_down[0], _core(w_down[0])

    place = jnp.stack([c, y, x, (y * 4 + x) * 2 + zl]).astype(jnp.int32)
    sel_own, sel_other, weight = _route(place, routes.T, gate_probs.T, slots)
    near = [_zh(pair, s) for s in SHIFTS]
    *near, sel_own = barrier((*near, sel_own))
    near = [pair] + near
    by_shift = {0: near[0], 1: near[1], 3: near[2], 2: near[3]}
    ordered = []
    for k in range(4):
        pick = by_shift[0]
        for s in SHIFTS:
            pick = jnp.where((zh - k) % 4 == s, by_shift[s], pick)
        ordered.append(pick)
    block = jnp.concatenate(ordered, 1)
    line = jnp.concatenate([block] + [_lines(block, s, True) for s in SHIFTS], 0)

    xr = x_rows[0]
    x_own = _dot(sel_own, xr, ((1,), (0,))).astype(BF)
    line, x_own, gates, ups = barrier((line, x_own, gates, ups))
    wg = jnp.concatenate(gates, 1)
    wu = jnp.concatenate(ups, 1)
    opposite = _lines(line, 2, False)
    gate_pre = _dot(x_own, wg, ((1,), (0,)))
    near_line, gate_pre = barrier((line, gate_pre))
    up_pre = _dot(x_own, wu, ((1,), (0,)))
    sigmoid_gate = jax.nn.sigmoid(gate_pre)
    activated = gate_pre * sigmoid_gate
    hidden = (activated * up_pre).astype(BF)
    slope = up_pre * sigmoid_gate * (1.0 + gate_pre * (1.0 - sigmoid_gate))
    sides = _lines(near_line, 1, False), _lines(near_line, 3, False)

    hidden_other = _core(hidden[:, ff:])

    args = weight, slope, activated, downs, gates, ups
    mine, rows, *kept = _pair_step(0, (line, opposite), *args, ())
    rows, hidden_other = barrier((rows, hidden_other))
    back = [_lines(rows, 2, False)]
    *rows, row_own, mid_own, mid_other = _pair_step(1, sides, *args, kept)
    back += [_lines(rows[0], 3, False), _lines(rows[1], 1, False)]

    row_other = _core(row_own)
    mid_other = _core(mid_other)
    keep, send = slice(0, 32), slice(32, None)
    kept_sum = mine[keep] + back[0][keep].astype(F32)
    sent_sum = mine[send] + back[0][send].astype(F32)
    kept_sum, sent_sum, mid_other = barrier((kept_sum, sent_sum, mid_other))
    grad_gate, grad_up = _input_grads(sel_own, sel_other, mid_own, mid_other, xr, ff)
    grad_down = _down_grad(hidden, hidden_other, row_own, row_other, ff)

    last, grad_gate, grad_up, grad_down = barrier((back[2], grad_gate, grad_up, grad_down))

    def added(total, part):
        return total + back[1][part].astype(F32) + last[part].astype(F32)

    result = added(kept_sum, keep)
    sent = added(sent_sum, send).astype(BF)
    for i, s in enumerate(SHIFTS):
        result = result + _lines(sent[32 * i : 32 * (i + 1)], -s, True).astype(F32)
    share = result.shape[1] // 4
    quarters = [result[:, k * share : (k + 1) * share] for k in range(4)]

    def for_zh(shift):
        pick = quarters[0]
        for k in range(1, 4):
            pick = jnp.where((zh + shift) % 4 == k, quarters[k], pick)
        return pick

    mine = for_zh(0)
    for s in SHIFTS:
        mine = mine + _zh(for_zh(s).astype(BF), s).astype(F32)
    halves = mine[:, : share // 2], mine[:, share // 2 :]
    same = jnp.where(c == 0, halves[0], halves[1])
    other = jnp.where(c == 0, halves[1], halves[0])
    got = _pair(jnp.where(home, other, same).astype(BF), CYCLE_BACK).astype(F32)
    far = _pair(other.astype(BF), ACROSS).astype(F32)
    grad_in = (jnp.where(home, same, far) + got).astype(BF)
    return grad_in, grad_gate[None], grad_up[None], grad_down[None]


def solution(mesh):
    fine = Mesh(mesh.devices.reshape(4, 2, 4, 4, 2), ("zh", "c", "y", "x", "zl"))
    expert, dp = ("y", "x", "zl"), ("zh", "c")
    placed = (
        P(expert, dp),
        P(),
        P(),
        P(expert, None, None),
        P(expert, None, dp),
        P(expert, None, dp),
        P(expert, dp, None),
    )
    return jax.shard_map(
        body,
        mesh=fine,
        in_specs=placed,
        out_specs=(
            P(expert, dp),
            P(expert, None, dp),
            P(expert, None, dp),
            P(expert, dp, None),
        ),
        check_vma=False,
    )
```
